512 devices in a mesh: wide: 128 (over z, y, core), mp: 4 (over x).
Axes of the slice: x: 4, y: 8, z: 8, core: 2. Of those that a mesh axis runs over, the one named last changes fastest.
Arguments:
- passage_states: bfloat16 [32768, 8192], P('wide', 'mp')
- norm_gain: float32 [8192], P('mp'), may hold values from 0.1 to 1.9
- proj_weight: bfloat16 [8192, 1024], P('mp', 'wide'), may hold values from -0.0625 to 0.0625
- query_states: bfloat16 [32768, 4096], P('wide', 'mp')
- self_keyvals: bfloat16 [32768, 1024], P('wide', 'mp')
- output_grads: bfloat16 [32768, 4096], P('wide', 'mp'), may hold values from -6 to 6
- passage_ids: int32 [256, 32], P('wide'), may hold values from -1 to 2047, as said below
- passage_counts: int32 [256], P('wide'), may hold values from 16 to 32, as said below
Outputs:
- state_grads: bfloat16 [32768, 8192], P('wide', 'mp')
- gain_grads: float32 [8192], P('mp')
- query_gradient: float32 [32768, 4096], P('wide', 'mp')
- self_keyval_grads: float32 [32768, 1024], P('wide', 'mp')
The draws below stay inside these ranges and needn't reach their ends.
Inputs may be any that keep to these rules, and one draw needn't show every extreme that they name: `passage_ids`: passage p lives on index p // 16 of wide. Row q names distinct passages in its first passage_counts[q] entries and holds -1 after them. The 2 questions of one index of wide name distinct passages and together read at most 1 passages that live on any one index of wide; that bound is reached in every draw. `passage_counts`: some question reads 32 passages in every draw.
All inputs are finite; a program needn't handle non-finite values.
Results may differ from the reference program's by a relative error of at most 0.012.
Values may be sent and summed in bfloat16 or wider, within the bound.
No kernel may reach another device: no remote copies, remote signals or barrier semaphores. Data moves between devices by JAX's collectives and lax.ppermute only.
A program may use at most 64 MiB of HBM per device.

```python
import math
import jax
import jax.numpy as jnp
from jax import lax

D = 8192
HD = 128
KVH = 4
GROUP = 8
MROWS = 16
QLEN = 128
Q_DEV = 2
CAP = 32
P_DEV = 16
HQ = 32
PASSAGES = 2048
PROWS = 32768
QUESTIONS = 256
TOKENS = 32768
REQS = 64
OWNERS = 64
SLOT = 1
N_WIDE = 128


def request_plan(key):
    subkeys = jax.random.split(jax.random.fold_in(key, 101), 4)
    drawn_counts = jax.random.randint(subkeys[0], (QUESTIONS,), CAP // 2, CAP + 1)
    forced = jax.random.randint(subkeys[1], (), 0, QUESTIONS)
    counts = jnp.where(jnp.arange(QUESTIONS) == forced, CAP, drawn_counts).astype(jnp.int32)
    device_total = QUESTIONS // Q_DEV
    owner_keys = jax.random.split(subkeys[2], device_total)
    shuffled = jax.vmap(lambda one_key: jax.random.permutation(one_key, device_total))(owner_keys)
    offsets = jax.random.randint(subkeys[3], (device_total, OWNERS), 0, P_DEV)
    request_pos = jnp.arange(REQS)
    block_index = request_pos // SLOT
    within = request_pos % SLOT
    owner_ids = shuffled[:, :OWNERS][:, block_index]
    local_ids = (offsets[:, block_index] + within[None, :]) % P_DEV
    passage_list = (owner_ids * P_DEV + local_ids).reshape(QUESTIONS, CAP)
    live = jnp.arange(CAP)[None, :] < counts[:, None]
    return (counts, jnp.where(live, passage_list, -1).astype(jnp.int32))


def self_base(key):
    return jax.random.normal(jax.random.fold_in(key, 7), (TOKENS, KVH * 2 * HD), jnp.float32)


def draw_passage_ids(key, part):
    planned = request_plan(key)
    return planned[1]


def draw_passage_counts(key, part):
    planned = request_plan(key)
    return planned[0]


def draw_self_keyvals(key, part):
    base = self_base(key)
    return base.astype(jnp.bfloat16)


def draw_query_states(key, part):
    key = jax.random.fold_in(key, 23)
    result = jax.random.normal(key, (TOKENS, HQ * HD), jnp.float32)
    return result.astype(jnp.bfloat16)


def column_trend(rise):
    columns = jnp.arange(D).astype(jnp.float32)
    return math.log(rise) * columns / D


def draw_passage_states(key, part):
    key = jax.random.fold_in(key, 41)
    subkeys = jax.random.split(key, 3)
    trend = column_trend(10.0)
    column_scale = jnp.exp(jax.random.uniform(subkeys[0], (D,), jnp.float32, 0.0, math.log(10.0)) + trend)
    row_scale = jnp.exp(jax.random.uniform(subkeys[1], (PROWS, 1), jnp.float32, 0.0, math.log(10.0)))
    base = jax.random.normal(subkeys[2], (PROWS, D), jnp.float32)
    return (base * column_scale[None, :] * row_scale).astype(jnp.bfloat16)


def block_levels(key, shape, shards, least, top_value):
    def one(dim, blocks):
        draws = jax.random.uniform(jax.random.fold_in(jax.random.fold_in(key, 6), dim), (blocks,), jnp.float32, least / len(shards), top_value / len(shards))
        return jnp.repeat(jnp.exp(draws), shape[dim] // blocks).reshape((-1,) + (1,) * (len(shape) - dim - 1))

    level = one(*shards[0])
    for cut in shards[1:]:
        level = level * one(*cut)
    return level


def scatter_about(stream_key, dims, scale, limit, cuts=(), kind=jnp.bfloat16):
    values = scale * jax.random.normal(stream_key, dims, jnp.float32)
    if cuts:
        values = values * block_levels(stream_key, dims, cuts, -0.22, 0.18)
    return jnp.clip(values, -limit, limit).astype(kind)


def setup_inputs(seed: int = 0) -> dict:
    arg_keys = jax.random.split(jax.random.key(seed), 9)
    passage_states = draw_passage_states(jax.random.fold_in(arg_keys[8], 71), 0)
    norm_gain = jnp.clip(1.0 + 0.18 * jax.random.normal(arg_keys[1], (D,), jnp.float32), 0.1, 1.9)
    proj_weight = scatter_about(arg_keys[2], (D, KVH * 2 * HD), D ** -0.5, 0.0625, ((0, 4), (1, 128)))
    query_states = draw_query_states(jax.random.fold_in(arg_keys[8], 71), 0)
    self_keyvals = draw_self_keyvals(jax.random.fold_in(arg_keys[8], 71), 0)
    output_grads = scatter_about(arg_keys[5], (TOKENS, HQ * HD), 1.0, 6.0, ((0, 128), (1, 4)))
    passage_ids = draw_passage_ids(jax.random.fold_in(arg_keys[8], 71), 0)
    passage_counts = draw_passage_counts(jax.random.fold_in(arg_keys[8], 71), 0)
    return dict(passage_states=passage_states, norm_gain=norm_gain, proj_weight=proj_weight, query_states=query_states, self_keyvals=self_keyvals, output_grads=output_grads, passage_ids=passage_ids, passage_counts=passage_counts)


epsilon = 1e-05
highest_score = lax.Precision.HIGHEST

def attend_all(query_rows, output_gradient, memory, self_rows, live_count):
    score_scale = 1.0 / math.sqrt(HD)
    mem_total = memory.shape[0]
    memory_key_rows = jnp.concatenate([memory[:, :, 0], self_rows[:, :, 0]], axis=0)
    memory_value_rows = jnp.concatenate([memory[:, :, 1], self_rows[:, :, 1]], axis=0)
    columns = jnp.arange(mem_total + QLEN)
    positions = jnp.arange(QLEN)
    allowed = jnp.where(columns[None, :] < mem_total, columns[None, :] < live_count * MROWS, columns[None, :] - mem_total <= positions[:, None])
    score_matrix = jnp.einsum('tycb,syb->ycts', query_rows, memory_key_rows, precision=highest_score) * score_scale
    score_matrix = jnp.where(allowed[None, None], score_matrix, -1e+30)
    score_matrix = score_matrix - lax.optimization_barrier(jnp.max(score_matrix, -1, keepdims=True))
    exponent = jnp.exp(score_matrix)
    probabilities = exponent / lax.optimization_barrier(jnp.sum(exponent, -1, keepdims=True))
    rounded_scores = lax.optimization_barrier(probabilities.astype(jnp.bfloat16)).astype(jnp.float32)
    attended_values = jnp.einsum('noar,rnb->anob', rounded_scores, memory_value_rows, precision=highest_score)
    row_delta = jnp.transpose(lax.optimization_barrier(jnp.sum(output_gradient * attended_values, -1)), (1, 2, 0))
    probability_gradient = jnp.einsum('tycb,syb->ycts', output_gradient, memory_value_rows, precision=highest_score)
    score_gradient = probabilities * (probability_gradient - row_delta[..., None]) * score_scale
    score_gradient = lax.optimization_barrier(score_gradient.astype(jnp.bfloat16)).astype(jnp.float32)
    query_gradient = jnp.einsum('noar,rnb->anob', score_gradient, memory_key_rows, precision=highest_score)
    key_gradient = jnp.einsum('wbeq,ewbo->qwo', score_gradient, query_rows, precision=highest_score)
    value_gradient = jnp.einsum('wbeq,ewbo->qwo', rounded_scores, output_gradient, precision=highest_score)
    both_grads = jnp.stack([key_gradient, value_gradient], axis=2)
    return (query_gradient, both_grads[mem_total:], both_grads[:mem_total].astype(jnp.bfloat16))

def reference(passage_states, norm_gain, proj_weight, query_states, self_keyvals, output_grads, passage_ids, passage_counts):
    state_blocks = passage_states.reshape(N_WIDE, P_DEV * MROWS, D)

    def forward_block(block_states):
        states = block_states.astype(jnp.float32)
        inverse_rms = lax.rsqrt(lax.optimization_barrier(jnp.mean(states * states, -1, keepdims=True)) + epsilon)
        memory_rows = (states * inverse_rms * norm_gain).astype(jnp.bfloat16)
        return jnp.dot(memory_rows, proj_weight, preferred_element_type=jnp.float32).astype(jnp.bfloat16)
    keyvals = lax.map(forward_block, state_blocks).reshape(PASSAGES, MROWS, KVH, 2, HD)

    def per_question(question_index):
        id_row = passage_ids[question_index]
        live_count = passage_counts[question_index]
        picked = jnp.take(keyvals, jnp.maximum(id_row, 0), axis=0)
        memory = picked.reshape(CAP * MROWS, KVH, 2, HD).astype(jnp.float32)
        first_row = (question_index * QLEN).astype(jnp.int32)
        query_rows = lax.dynamic_slice_in_dim(query_states, first_row, QLEN, 0).astype(jnp.float32).reshape(QLEN, KVH, GROUP, HD)
        output_gradient = lax.dynamic_slice_in_dim(output_grads, first_row, QLEN, 0).astype(jnp.float32).reshape(QLEN, KVH, GROUP, HD)
        self_rows = lax.dynamic_slice_in_dim(self_keyvals, first_row, QLEN, 0).astype(jnp.float32).reshape(QLEN, KVH, 2, HD)
        query_part, self_part, memory_part = attend_all(query_rows, output_gradient, memory, self_rows, live_count)
        return (query_part.reshape(QLEN, HQ * HD), self_part.reshape(QLEN, KVH * 2 * HD), memory_part.reshape(CAP, MROWS * KVH * 2 * HD))
    query_all, self_all, memory_all = lax.map(per_question, jnp.arange(QUESTIONS, dtype=jnp.int32))
    is_live = (passage_ids >= 0).astype(jnp.float32)
    contributions = (memory_all.astype(jnp.float32) * is_live[:, :, None]).reshape(QUESTIONS * CAP, MROWS * KVH * 2 * HD)
    passage_sums = jnp.zeros((PASSAGES, MROWS * KVH * 2 * HD), jnp.float32).at[jnp.maximum(passage_ids, 0).reshape(-1)].add(contributions)
    passage_grads = passage_sums.astype(jnp.bfloat16).reshape(N_WIDE, P_DEV * MROWS, KVH * 2 * HD)

    def backward_block(block_items):
        block_grads, block_states = block_items
        states = block_states.astype(jnp.float32)
        inverse_rms = lax.rsqrt(lax.optimization_barrier(jnp.mean(states * states, -1, keepdims=True)) + epsilon)
        normed = states * inverse_rms
        row_grads = jnp.dot(block_grads, proj_weight.T, preferred_element_type=jnp.float32)
        scaled_grads = row_grads * norm_gain
        row_mean = lax.optimization_barrier(jnp.mean(scaled_grads * normed, -1, keepdims=True))
        state_part = (inverse_rms * (scaled_grads - normed * row_mean)).astype(jnp.bfloat16)
        return (state_part, lax.optimization_barrier(jnp.sum(row_grads * normed, 0)))
    state_grads, gain_parts = lax.map(backward_block, (passage_grads, state_blocks))
    return (state_grads.reshape(PROWS, D), lax.optimization_barrier(jnp.sum(gain_parts, 0)), query_all.reshape(TOKENS, HQ * HD), self_all.reshape(TOKENS, KVH * 2 * HD))
```

```python
import math

import jax
import jax.numpy as jnp
from jax import lax
from jax.experimental import pallas as pl
from jax.experimental.pallas import tpu as pltpu
from jax.sharding import Mesh
from jax.sharding import PartitionSpec as P

D = 8192
MROWS = 16
HEAD = 128
GROUP = 8
QLEN = 128
CAP = 32
MEM = CAP * MROWS
KEYS = MEM + QLEN
N_WIDE = 128
P_DEV = 16
EPSILON = 1e-05
SCALE = 1.0 / math.sqrt(HEAD)
LOG2E = math.log2(math.e)
VMEM_LIMIT = 48 * 1024 * 1024

NT = (((1,), (1,)), ((), ()))
TN = (((0,), (0,)), ((), ()))


def dot(a, b, dims=(((1,), (0,)), ((), ()))):
    return lax.dot_general(a, b, dims, preferred_element_type=jnp.float32)


def params():
    return pltpu.CompilerParams(vmem_limit_bytes=VMEM_LIMIT)


def whole(shape):
    return pl.BlockSpec(shape, lambda *_: (0,) * len(shape))


def project_kernel(rows_ref, weight_ref, out_ref):
    out_ref[0] = dot(rows_ref[...], weight_ref[...], NT).astype(out_ref.dtype)


def project(rows, blob, dtype):
    row_total, depth = rows.shape
    heads = blob.shape[0] // (2 * HEAD)
    return pl.pallas_call(
        project_kernel,
        grid=(heads,),
        in_specs=[
            whole((row_total, depth)),
            pl.BlockSpec((2 * HEAD, depth), lambda h: (h, 0)),
        ],
        out_specs=pl.BlockSpec((1, row_total, 2 * HEAD), lambda h: (h, 0, 0)),
        out_shape=jax.ShapeDtypeStruct((heads, row_total, 2 * HEAD), dtype),
        compiler_params=params(),
        cost_estimate=pl.CostEstimate(
            flops=2 * row_total * depth * heads * 2 * HEAD, bytes_accessed=4 << 20, transcendentals=0
        ),
    )(rows, blob)


def pack_kernel(wanted_ref, parts_ref, out_ref, keyvals_ref, table_ref):
    total = parts_ref[0].astype(jnp.float32)
    for part in range(1, parts_ref.shape[0]):
        total = total + parts_ref[part].astype(jnp.float32)
    total = total.reshape(P_DEV, MROWS, 2 * HEAD)
    keyvals_ref[...] = total
    table_ref[...] = total.astype(jnp.bfloat16)
    for slot in range(N_WIDE):
        out_ref[slot] = table_ref[jnp.maximum(wanted_ref[slot], 0)]


def pack(wanted, parts):
    table = (P_DEV, MROWS, 2 * HEAD)
    outgoing = (N_WIDE, MROWS, 2 * HEAD)
    return pl.pallas_call(
        pack_kernel,
        grid_spec=pltpu.PrefetchScalarGridSpec(
            num_scalar_prefetch=1,
            grid=(1,),
            in_specs=[whole(parts.shape)],
            out_specs=[whole(outgoing), whole(table)],
            scratch_shapes=[pltpu.VMEM(table, jnp.bfloat16)],
        ),
        out_shape=[
            jax.ShapeDtypeStruct(outgoing, jnp.bfloat16),
            jax.ShapeDtypeStruct(table, jnp.float32),
        ],
        compiler_params=params(),
        cost_estimate=pl.CostEstimate(flops=1 << 20, bytes_accessed=2 << 20, transcendentals=0),
    )(wanted, parts)


def attend_kernel(
    owners_ref,
    counts_ref,
    arrived_ref,
    query_ref,
    grad_ref,
    self_ref,
    query_out,
    self_out,
    outgoing_ref,
    key_rows,
    value_rows,
    key_grads,
    value_grads,
):
    question = pl.program_id(0)
    live = counts_ref[question]

    @pl.when(question == 0)
    def _():
        outgoing_ref[...] = jnp.zeros_like(outgoing_ref)

    for k in range(CAP):
        owner = owners_ref[question * CAP + k]
        rows = pl.ds(k * MROWS, MROWS)
        key_rows[rows, :] = arrived_ref[owner, :, :HEAD]
        value_rows[rows, :] = arrived_ref[owner, :, HEAD:]
    key_rows[MEM:, :] = self_ref[:, :HEAD]
    value_rows[MEM:, :] = self_ref[:, HEAD:]
    key_block = key_rows[...]
    value_block = value_rows[...]
    key_turned = key_block.T
    pair = 2 * QLEN
    key_index = lax.broadcasted_iota(jnp.int32, (MEM, pair), 0)
    self_index = lax.broadcasted_iota(jnp.int32, (QLEN, pair), 0)
    token = lax.broadcasted_iota(jnp.int32, (QLEN, pair), 1) % QLEN
    allowed = jnp.concatenate([key_index < live * MROWS, self_index <= token], axis=0)
    for g in range(0, GROUP, 2):
        first = slice(g * HEAD, (g + 1) * HEAD)
        second = slice((g + 1) * HEAD, (g + 2) * HEAD)
        queries = jnp.concatenate([query_ref[:, first], query_ref[:, second]], axis=0)
        grads = jnp.concatenate([grad_ref[:, first], grad_ref[:, second]], axis=0)
        scores = jnp.where(allowed, dot(key_block, queries, NT), -1e30)
        top = jnp.max(scores, axis=0, keepdims=True)
        exponent = jnp.exp2((scores - top) * (SCALE * LOG2E))
        probs = exponent * (1.0 / jnp.sum(exponent, axis=0, keepdims=True))
        rounded = probs.astype(jnp.bfloat16)
        prob_grads = dot(value_block, grads, NT)
        delta = jnp.sum(rounded.astype(jnp.float32) * prob_grads, axis=0, keepdims=True)
        score_grads = (probs * (prob_grads - delta) * SCALE).astype(jnp.bfloat16)
        value_part = dot(rounded, grads)
        key_part = dot(score_grads, queries)
        if g == 0:
            value_grads[...] = value_part
            key_grads[...] = key_part
        else:
            value_grads[...] += value_part
            key_grads[...] += key_part
        query_part = dot(key_turned, score_grads)
        query_out[:, first] = query_part[:, :QLEN].T
        query_out[:, second] = query_part[:, QLEN:].T
    self_out[:, :HEAD] = key_grads[MEM:, :]
    self_out[:, HEAD:] = value_grads[MEM:, :]
    for k in range(CAP):
        owner = owners_ref[question * CAP + k]
        rows = pl.ds(k * MROWS, MROWS)

        @pl.when(k < live)
        def _():
            outgoing_ref[owner, :, :HEAD] = key_grads[rows, :].astype(jnp.bfloat16)
            outgoing_ref[owner, :, HEAD:] = value_grads[rows, :].astype(jnp.bfloat16)


def attend(owners, counts, arrived, queries, grads, self_rows):
    token_total, width = queries.shape
    row_width = self_rows.shape[1]
    questions = token_total // QLEN

    def per_question(columns):
        return pl.BlockSpec((QLEN, columns), lambda q, *_: (q, 0))

    return pl.pallas_call(
        attend_kernel,
        grid_spec=pltpu.PrefetchScalarGridSpec(
            num_scalar_prefetch=2,
            grid=(questions,),
            in_specs=[
                whole(arrived.shape),
                per_question(width),
                per_question(width),
                per_question(row_width),
            ],
            out_specs=[per_question(width), per_question(row_width), whole(arrived.shape)],
            scratch_shapes=[
                pltpu.VMEM((KEYS, HEAD), jnp.bfloat16),
                pltpu.VMEM((KEYS, HEAD), jnp.bfloat16),
                pltpu.VMEM((KEYS, HEAD), jnp.float32),
                pltpu.VMEM((KEYS, HEAD), jnp.float32),
            ],
        ),
        out_shape=[
            jax.ShapeDtypeStruct((token_total, width), jnp.float32),
            jax.ShapeDtypeStruct((token_total, row_width), jnp.float32),
            jax.ShapeDtypeStruct(arrived.shape, jnp.bfloat16),
        ],
        compiler_params=params(),
        cost_estimate=pl.CostEstimate(
            flops=2 << 30, bytes_accessed=5 << 20, transcendentals=questions * GROUP * QLEN * KEYS
        ),
    )(owners, counts, arrived, queries, grads, self_rows)


def collect_kernel(wanted_ref, returned_ref, keyvals_ref, out_ref, sums):
    sums[...] = jnp.zeros_like(sums)
    for slot in range(N_WIDE):
        row = wanted_ref[slot]
        place = jnp.where(row < 0, P_DEV, row)
        sums[place] += returned_ref[slot].astype(jnp.float32)
    total = P_DEV * MROWS
    rounded = sums[:P_DEV].reshape(total, 2 * HEAD).astype(jnp.bfloat16)
    out_ref[:total, :] = rounded
    products = rounded.astype(jnp.float32) * keyvals_ref[...].reshape(total, 2 * HEAD)
    inner = lax.dot_general(
        jnp.ones((8, 2 * HEAD), jnp.float32),
        products,
        NT,
        precision=lax.Precision.HIGHEST,
        preferred_element_type=jnp.float32,
    )
    high = inner.astype(jnp.bfloat16)
    low = (inner - high.astype(jnp.float32)).astype(jnp.bfloat16)
    out_ref[total:, :] = jnp.concatenate([high, low], axis=0)


def collect(wanted, returned, keyvals):
    out = (P_DEV * MROWS + 16, 2 * HEAD)
    return pl.pallas_call(
        collect_kernel,
        grid_spec=pltpu.PrefetchScalarGridSpec(
            num_scalar_prefetch=1,
            grid=(1,),
            in_specs=[whole(returned.shape), whole(keyvals.shape)],
            out_specs=whole(out),
            scratch_shapes=[pltpu.VMEM((P_DEV + 1, MROWS, 2 * HEAD), jnp.float32)],
        ),
        out_shape=jax.ShapeDtypeStruct(out, jnp.bfloat16),
        compiler_params=params(),
        cost_estimate=pl.CostEstimate(flops=1 << 20, bytes_accessed=2 << 20, transcendentals=0),
    )(wanted, returned, keyvals)


def finish_kernel(
    all_heads_ref, weight_ref, states_ref, gain_ref, inverse_ref, out_ref, gain_out, mean_ref
):
    heads = all_heads_ref.shape[0]
    total = states_ref.shape[0]

    @pl.when(pl.program_id(0) == 0)
    def _():
        extra = jnp.concatenate([all_heads_ref[h, total:, :] for h in range(heads)], axis=0)
        share = jnp.full((extra.shape[0], HEAD), 1.0 / (8 * D), jnp.bfloat16)
        mean_ref[...] = dot(extra, share, TN)

    weight = weight_ref[0]
    row_grads = dot(all_heads_ref[0, :total, :], weight[: 2 * HEAD, :])
    for h in range(1, heads):
        row_grads += dot(
            all_heads_ref[h, :total, :], weight[h * 2 * HEAD : (h + 1) * 2 * HEAD, :]
        )
    inverse = inverse_ref[:, :1]
    normed = states_ref[...].astype(jnp.float32) * inverse
    gain_out[...] = jnp.sum(row_grads * normed, axis=0, keepdims=True)
    out_ref[...] = (
        inverse * (row_grads * gain_ref[...] - normed * mean_ref[:, :1])
    ).astype(jnp.bfloat16)


def finish(all_heads, weights, states, gain, inverse):
    row_total, features = states.shape
    columns = weights.shape[1]
    halves = weights.shape[0]
    block = 256
    per_half = features // halves // block
    return pl.pallas_call(
        finish_kernel,
        grid=(features // block,),
        in_specs=[
            whole(all_heads.shape),
            pl.BlockSpec((1, columns, block), lambda b: (b // per_half, 0, b % per_half)),
            pl.BlockSpec((row_total, block), lambda b: (0, b)),
            pl.BlockSpec((1, block), lambda b: (0, b)),
            whole(inverse.shape),
        ],
        out_specs=[
            pl.BlockSpec((row_total, block), lambda b: (0, b)),
            pl.BlockSpec((1, block), lambda b: (0, b)),
        ],
        out_shape=[
            jax.ShapeDtypeStruct((row_total, features), jnp.bfloat16),
            jax.ShapeDtypeStruct((1, features), jnp.float32),
        ],
        scratch_shapes=[pltpu.VMEM((row_total, HEAD), jnp.float32)],
        compiler_params=params(),
        cost_estimate=pl.CostEstimate(
            flops=2 * row_total * features * columns, bytes_accessed=7 << 20, transcendentals=0
        ),
    )(all_heads, weights, states, gain, inverse)


def spread(array, axis):
    count = lax.axis_size(axis)
    copies = jnp.broadcast_to(array[None], (count,) + array.shape)
    return lax.all_to_all(copies, axis, 0, 0, tiled=True)


SWAP = ((0, 1), (1, 0))


def on_device(
    passage_states,
    norm_gain,
    proj_weight,
    query_states,
    self_keyvals,
    output_grads,
    passage_ids,
    passage_counts,
):
    wide = ("z", "y", "c")
    core = lax.axis_index("c")
    me = lax.axis_index(wide)
    half = passage_states.shape[1] // 2

    live = jnp.arange(CAP, dtype=jnp.int32)[None, :] < passage_counts[:, None]
    owners = jnp.where(live, passage_ids // P_DEV, 0).reshape(-1)
    places = jnp.where(live, passage_ids % P_DEV + 1, 0).reshape(-1)
    hits = owners[:, None] == jnp.arange(N_WIDE)[None, :]
    requests = jnp.sum(jnp.where(hits, places[:, None], 0), 0).astype(jnp.bfloat16)

    turned = proj_weight.T
    columns = turned.shape[0]
    halves = jnp.transpose(turned.reshape(columns, 2, half), (1, 0, 2))
    ridden = jnp.broadcast_to(requests[None, None], (2, columns, N_WIDE))
    blob = jnp.concatenate([halves, ridden], axis=2)
    blob = lax.all_to_all(blob, "c", 0, 0, tiled=True).reshape(2 * columns, half + N_WIDE)
    blob = spread(blob, "y").reshape(-1, half + N_WIDE)
    blob, passage_states = lax.optimization_barrier((blob, passage_states))
    blob = lax.all_gather(blob, "z", axis=0, tiled=True)

    states = passage_states.astype(jnp.float32)
    squares = lax.psum(jnp.sum(states * states, 1), "mp")
    inverse_rms = lax.rsqrt(squares / D + EPSILON)[:, None]
    memory_rows = (states * inverse_rms * norm_gain).astype(jnp.bfloat16)
    own_rows = lax.dynamic_slice_in_dim(memory_rows, core * half, half, 1)
    give_rows = lax.dynamic_slice_in_dim(memory_rows, (1 - core) * half, half, 1)
    got_rows = lax.ppermute(give_rows, "c", SWAP)

    wanted = blob.reshape(N_WIDE, columns, -1)[:, 0, half:].astype(jnp.int32)
    wanted = jnp.sum(jnp.where(jnp.arange(N_WIDE)[None, :] == me, wanted, 0), 1) - 1

    give_sums = project(got_rows, blob, jnp.bfloat16)
    got_sums = lax.ppermute(give_sums, "c", SWAP)
    own_sums = project(own_rows, blob, jnp.float32)
    partial_sums = (own_sums + got_sums.astype(jnp.float32)).astype(jnp.bfloat16)
    parts = lax.all_to_all(partial_sums, "mp", 0, 0, tiled=True)
    outgoing, keyvals = pack(wanted, parts)
    arrived = lax.all_to_all(outgoing, wide, 0, 0, tiled=True)
    weights = lax.all_gather(blob, "c", axis=0, tiled=False)

    query_gradient, self_keyval_grads, memory_grads = attend(
        owners, passage_counts, arrived, query_states, output_grads, self_keyvals
    )
    returned = lax.all_to_all(memory_grads, wide, 0, 0, tiled=True)
    passage_grads = collect(wanted, returned, keyvals)
    all_heads = spread(passage_grads, "mp").reshape((-1,) + passage_grads.shape)
    inverse_wide = jnp.broadcast_to(inverse_rms, (inverse_rms.shape[0], HEAD))
    state_grads, gain_part = finish(
        all_heads, weights, passage_states, norm_gain[None, :], inverse_wide
    )
    gain_part = lax.psum(gain_part.reshape(-1, HEAD), "c")
    gain_part = jnp.sum(spread(gain_part, "y").reshape(8, -1, HEAD), 0)
    gain_grads = jnp.sum(spread(gain_part, "z").reshape(8, -1), 0)
    return (state_grads, gain_grads, query_gradient, self_keyval_grads)


def solution(mesh):
    grid = Mesh(mesh.devices.reshape(8, 8, 2, 4), ("z", "y", "c", "mp"))
    wide = ("z", "y", "c")
    in_specs = (
        P(wide, "mp"),
        P("mp"),
        P("mp", wide),
        P(wide, "mp"),
        P(wide, "mp"),
        P(wide, "mp"),
        P(wide, None),
        P(wide),
    )
    out_specs = (P(wide, "mp"), P("mp"), P(wide, "mp"), P(wide, "mp"))
    return jax.shard_map(
        on_device, mesh=grid, in_specs=in_specs, out_specs=out_specs, check_vma=False
    )
```

```python
import math

import jax
import jax.numpy as jnp
from jax import lax
from jax.experimental import pallas as pl
from jax.experimental.pallas import tpu as pltpu
from jax.sharding import Mesh
from jax.sharding import PartitionSpec as P

D = 8192
MROWS = 16
HEAD = 128
GROUP = 8
QLEN = 128
CAP = 32
MEM = CAP * MROWS
KEYS = MEM + QLEN
N_WIDE = 128
P_DEV = 16
EPSILON = 1e-05
SCALE = 1.0 / math.sqrt(HEAD)
LOG2E = math.log2(math.e)
FEW, MANY = 32 * 1024 * 1024, 60 * 1024 * 1024

NT = (((1,), (1,)), ((), ()))
TN = (((0,), (0,)), ((), ()))
SWAP = ((0, 1), (1, 0))
VMEM = pl.BlockSpec(memory_space=pltpu.VMEM)
SMEM = pl.BlockSpec(memory_space=pltpu.SMEM)
HBM = pl.BlockSpec(memory_space=pltpu.HBM)


def dot(a, b, dims=(((1,), (0,)), ((), ()))):
    return lax.dot_general(a, b, dims, preferred_element_type=jnp.float32)


def kernel_call(
    body, scalars, arrays, out_shapes, scratch=(), flops=1 << 20, moved=2 << 20, given=VMEM, out=VMEM, limit=MANY
):
    return pl.pallas_call(
        body,
        in_specs=[SMEM] * len(scalars) + [given] * len(arrays),
        out_specs=[out] * len(out_shapes),
        out_shape=[jax.ShapeDtypeStruct(*one) for one in out_shapes],
        scratch_shapes=list(scratch),
        compiler_params=pltpu.CompilerParams(vmem_limit_bytes=limit),
        cost_estimate=pl.CostEstimate(flops=flops, bytes_accessed=moved, transcendentals=0),
    )(*scalars, *arrays)


def wide_as(columns, width):
    return jnp.concatenate([columns] * (width // columns.shape[1]), axis=1)


def project_kernel(place_ref, rows_ref, weight_ref, *refs):
    *others, out_ref = refs
    half = rows_ref.shape[1] // 2
    rows = rows_ref[:, pl.ds(pl.multiple_of(place_ref[0] * half, half), half)]
    for h in range(out_ref.shape[0]):
        total = dot(rows, weight_ref[h * 2 * HEAD : (h + 1) * 2 * HEAD, :half], NT)
        for other in others:
            total = total + other[h]
        out_ref[h] = total.astype(out_ref.dtype)


def project(place, rows, weight, dtype, *others):
    shape = (weight.shape[0] // (2 * HEAD), rows.shape[0], 2 * HEAD)
    (sums,) = kernel_call(
        project_kernel,
        (place,),
        (rows, weight) + others,
        [(shape, dtype)],
        flops=1 << 29,
        moved=4 << 20,
        limit=FEW,
    )
    return sums


PACK_STEPS = 4


def pack_kernel(
    wanted_ref,
    parts_ref,
    out_hbm,
    keyvals_hbm,
    out_ref,
    keyvals_ref,
    table_ref,
    sems,
):
    total = parts_ref[0].astype(jnp.float32)
    for part in range(1, parts_ref.shape[0]):
        total = total + parts_ref[part].astype(jnp.float32)
    total = total.reshape(P_DEV, MROWS, 2 * HEAD)
    keyvals_ref[...] = total
    copies = [pltpu.make_async_copy(keyvals_ref, keyvals_hbm, sems.at[PACK_STEPS])]
    copies[0].start()
    table_ref[...] = total.astype(jnp.bfloat16)
    slots = N_WIDE // PACK_STEPS
    for step in range(PACK_STEPS):
        for slot in range(step * slots, (step + 1) * slots):
            out_ref[slot] = table_ref[jnp.maximum(wanted_ref[slot], 0)]
        done = pl.ds(step * slots, slots)
        copies.append(pltpu.make_async_copy(out_ref.at[done], out_hbm.at[done], sems.at[step]))
        copies[-1].start()
    for copy in copies:
        copy.wait()


def attend_kernel(
    slots_ref,
    arrived_hbm,
    query_hbm,
    grad_hbm,
    self_hbm,
    query_out_hbm,
    self_out_hbm,
    outgoing_hbm,
    arrived_ref,
    query_ref,
    grad_ref,
    self_ref,
    query_out,
    self_out,
    outgoing_ref,
    key_rows,
    value_rows,
    key_grads,
    value_grads,
    in_sems,
    out_sems,
    question_sems,
):
    loads = [
        pltpu.make_async_copy(source, target, in_sems.at[index])
        for index, (source, target) in enumerate(
            [
                (arrived_hbm, arrived_ref),
                (query_hbm, query_ref),
                (grad_hbm, grad_ref),
                (self_hbm, self_ref),
            ]
        )
    ]
    for load in loads:
        load.start()
    outgoing_ref[...] = jnp.zeros_like(outgoing_ref)
    for load in loads:
        load.wait()
    pair = 2 * QLEN
    key_index = lax.broadcasted_iota(jnp.int32, (MEM, pair), 0)
    self_index = lax.broadcasted_iota(jnp.int32, (QLEN, pair), 0)
    token = lax.broadcasted_iota(jnp.int32, (QLEN, pair), 1) % QLEN

    @pl.loop(0, query_ref.shape[0] // QLEN)
    def _(question):
        live = slots_ref[SLOTS + question]
        tokens = pl.ds(pl.multiple_of(question * QLEN, QLEN), QLEN)
        for k in range(CAP):
            slot = slots_ref[question * CAP + k]
            key_rows[k * MROWS : (k + 1) * MROWS, :] = arrived_ref[slot, :, :HEAD]
            value_rows[k * MROWS : (k + 1) * MROWS, :] = arrived_ref[slot, :, HEAD:]
        key_rows[MEM:, :] = self_ref[tokens, :HEAD]
        value_rows[MEM:, :] = self_ref[tokens, HEAD:]
        key_block = key_rows[...]
        value_block = value_rows[...]
        key_turned = key_block.T
        allowed = jnp.concatenate([key_index < live * MROWS, self_index <= token], axis=0)
        for g in range(0, GROUP, 2):
            first = slice(g * HEAD, (g + 1) * HEAD)
            second = slice((g + 1) * HEAD, (g + 2) * HEAD)
            queries = jnp.concatenate([query_ref[tokens, first], query_ref[tokens, second]], axis=0)
            grads = jnp.concatenate([grad_ref[tokens, first], grad_ref[tokens, second]], axis=0)
            scores = jnp.where(allowed, dot(key_block, queries, NT), -1e30)
            top = jnp.max(scores, axis=0, keepdims=True)
            exponent = jnp.exp2((scores - top) * (SCALE * LOG2E))
            probs = exponent * (1.0 / jnp.sum(exponent, axis=0, keepdims=True))
            rounded = probs.astype(jnp.bfloat16)
            prob_grads = dot(value_block, grads, NT)
            delta = jnp.sum(rounded.astype(jnp.float32) * prob_grads, axis=0, keepdims=True)
            score_grads = (probs * (prob_grads - delta) * SCALE).astype(jnp.bfloat16)
            value_part = dot(rounded, grads)
            key_part = dot(score_grads, queries)
            if g == 0:
                value_grads[...] = value_part
                key_grads[...] = key_part
            else:
                value_grads[...] += value_part
                key_grads[...] += key_part
            query_part = dot(key_turned, score_grads)
            query_out[tokens, first] = query_part[:, :QLEN].T
            query_out[tokens, second] = query_part[:, QLEN:].T
        pltpu.make_async_copy(
            query_out.at[tokens], query_out_hbm.at[tokens], question_sems.at[question]
        ).start()
        self_out[tokens, :HEAD] = key_grads[MEM:, :]
        self_out[tokens, HEAD:] = value_grads[MEM:, :]
        for k in range(CAP):
            slot = slots_ref[question * CAP + k]
            rows = slice(k * MROWS, (k + 1) * MROWS)

            @pl.when(k < live)
            def _():
                outgoing_ref[slot, :, :HEAD] = key_grads[rows, :].astype(jnp.bfloat16)
                outgoing_ref[slot, :, HEAD:] = value_grads[rows, :].astype(jnp.bfloat16)

    stores = [
        pltpu.make_async_copy(outgoing_ref, outgoing_hbm, out_sems.at[0]),
        pltpu.make_async_copy(self_out, self_out_hbm, out_sems.at[1]),
    ]
    for store in stores:
        store.start()
    for question in range(query_ref.shape[0] // QLEN):
        tokens = pl.ds(question * QLEN, QLEN)
        stores.append(
            pltpu.make_async_copy(
                query_out.at[tokens], query_out_hbm.at[tokens], question_sems.at[question]
            )
        )
    for store in stores:
        store.wait()


def attend(slots, arrived, queries, grads, self_rows):
    return kernel_call(
        attend_kernel,
        (slots,),
        (arrived, queries, grads, self_rows),
        [
            (queries.shape, jnp.float32),
            (self_rows.shape, jnp.float32),
            (arrived.shape, jnp.bfloat16),
        ],
        [
            pltpu.VMEM(arrived.shape, jnp.bfloat16),
            pltpu.VMEM(queries.shape, jnp.bfloat16),
            pltpu.VMEM(grads.shape, jnp.bfloat16),
            pltpu.VMEM(self_rows.shape, jnp.bfloat16),
            pltpu.VMEM(queries.shape, jnp.float32),
            pltpu.VMEM(self_rows.shape, jnp.float32),
            pltpu.VMEM(arrived.shape, jnp.bfloat16),
        ]
        + [pltpu.VMEM((KEYS, HEAD), jnp.bfloat16)] * 2
        + [pltpu.VMEM((KEYS, HEAD), jnp.float32)] * 2
        + [pltpu.SemaphoreType.DMA((4,)), pltpu.SemaphoreType.DMA((2,)), pltpu.SemaphoreType.DMA((2,))],
        flops=2 << 30,
        moved=5 << 20,
        given=HBM,
        out=HBM,
    )


def collect_kernel(wanted_ref, returned_ref, keyvals_ref, out_ref, sums):
    sums[...] = jnp.zeros_like(sums)
    for slot in range(N_WIDE):
        row = wanted_ref[slot]
        sums[jnp.where(row < 0, P_DEV, row)] += returned_ref[slot].astype(jnp.float32)
    total = P_DEV * MROWS
    rounded = sums[:P_DEV].reshape(total, 2 * HEAD).astype(jnp.bfloat16)
    products = rounded.astype(jnp.float32) * keyvals_ref[...].reshape(total, 2 * HEAD)
    inner = lax.dot_general(
        jnp.ones((8, 2 * HEAD), jnp.float32),
        products,
        NT,
        precision=lax.Precision.HIGHEST,
        preferred_element_type=jnp.float32,
    )
    high = inner.astype(jnp.bfloat16)
    low = (inner - high.astype(jnp.float32)).astype(jnp.bfloat16)
    out_ref[:total, :] = rounded
    out_ref[total:, :] = jnp.concatenate([high, low], axis=0)


BLOCK = 256


def row_blocks(place_ref, all_heads_ref, weight_refs, states_ref, inverse_ref, finish):
    core = place_ref[0]
    total, features = states_ref.shape
    half = features // 2
    inverse = wide_as(inverse_ref[...], BLOCK)
    for place in range(2):
        start = (core if place == 0 else 1 - core) * half
        for block in range(half // BLOCK):
            span = slice(block * BLOCK, (block + 1) * BLOCK)
            row_grads = None
            for h in range(all_heads_ref.shape[0]):
                weight = weight_refs[place][h * 2 * HEAD : (h + 1) * 2 * HEAD, span]
                part = dot(all_heads_ref[h, :total, :], weight)
                row_grads = part if row_grads is None else row_grads + part
            lanes = pl.ds(pl.multiple_of(start + block * BLOCK, BLOCK), BLOCK)
            normed = states_ref[:, lanes].astype(jnp.float32) * inverse
            finish(lanes, row_grads, normed, inverse)


def gain_kernel(place_ref, all_heads_ref, w0, w1, states_ref, inverse_ref, out_ref):
    def finish(lanes, row_grads, normed, inverse):
        out_ref[:, lanes] = jnp.sum(row_grads * normed, axis=0, keepdims=True)

    row_blocks(place_ref, all_heads_ref, (w0, w1), states_ref, inverse_ref, finish)


def state_kernel(place_ref, all_heads_ref, w0, w1, states_ref, inverse_ref, gain_ref, out_ref):
    total = states_ref.shape[0]
    heads = all_heads_ref.shape[0]
    extra = jnp.concatenate([all_heads_ref[h, total:, :] for h in range(heads)], axis=0)
    share = jnp.full((extra.shape[0], HEAD), 1.0 / (8 * D), jnp.bfloat16)
    mean = wide_as(dot(extra, share, TN), BLOCK)

    def finish(lanes, row_grads, normed, inverse):
        scaled = row_grads * gain_ref[:, lanes]
        out_ref[:, lanes] = (inverse * (scaled - normed * mean)).astype(jnp.bfloat16)

    row_blocks(place_ref, all_heads_ref, (w0, w1), states_ref, inverse_ref, finish)


def spread(array, axis):
    count = lax.axis_size(axis)
    copies = jnp.broadcast_to(array[None], (count,) + array.shape)
    return lax.all_to_all(copies, axis, 0, 0, tiled=True)


WIDE = ("z", "y", "c")
SLOTS = 2 * CAP


def on_device(
    passage_states,
    norm_gain,
    proj_weight,
    query_states,
    self_keyvals,
    output_grads,
    passage_ids,
    passage_counts,
):
    core = lax.axis_index("c")
    place = jnp.stack([core, 1 - core]).astype(jnp.int32)
    me = lax.axis_index(WIDE)
    half = passage_states.shape[1] // 2

    live = jnp.arange(CAP, dtype=jnp.int32)[None, :] < passage_counts[:, None]
    owners = jnp.where(live, passage_ids // P_DEV, 0).reshape(-1)
    places = jnp.where(live, passage_ids % P_DEV + 1, 0).reshape(-1)
    hits = owners[:, None] == jnp.arange(N_WIDE)[None, :]
    requests = jnp.sum(jnp.where(hits, places[:, None], 0), 0).astype(jnp.bfloat16)

    turned = proj_weight.T
    columns = turned.shape[0]
    halves = jnp.transpose(turned.reshape(columns, 2, half), (1, 0, 2))
    ridden = jnp.broadcast_to(requests[None, None], (2, columns, N_WIDE))
    blob = jnp.concatenate([halves, ridden], axis=2)
    blob = lax.all_to_all(blob, "c", 0, 0, tiled=True).reshape(2 * columns, half + N_WIDE)
    blob = spread(blob, "y").reshape(-1, half + N_WIDE)
    blob, passage_states = lax.optimization_barrier((blob, passage_states))
    blob = lax.all_gather(blob, "z", axis=0, tiled=True)

    states = passage_states.astype(jnp.float32)
    squares = lax.psum(jnp.sum(states * states, 1), "mp")
    inverse_rms = lax.rsqrt(squares / D + EPSILON)[:, None]
    memory_rows = (states * inverse_rms * norm_gain).astype(jnp.bfloat16)
    inverse = jnp.broadcast_to(inverse_rms, (inverse_rms.shape[0], HEAD))
    weight, memory_rows, inverse = lax.optimization_barrier((blob, memory_rows, inverse))

    other_weight = lax.ppermute(weight, "c", SWAP)
    own_sums = project(place, memory_rows, weight, jnp.float32)
    partial_sums = project(place[::-1], memory_rows, other_weight, jnp.bfloat16, own_sums)
    wanted = weight.reshape(N_WIDE, columns, -1)[:, 0, half:].astype(jnp.int32)
    wanted = jnp.sum(jnp.where(jnp.arange(N_WIDE)[None, :] == me, wanted, 0), 1) - 1
    partial_sums, wanted = lax.optimization_barrier((partial_sums, wanted))
    parts = lax.all_to_all(partial_sums, "mp", 0, 0, tiled=True)
    table = (P_DEV, MROWS, 2 * HEAD)
    outgoing, keyvals = kernel_call(
        pack_kernel,
        (wanted,),
        (parts,),
        [((N_WIDE, MROWS, 2 * HEAD), jnp.bfloat16), (table, jnp.float32)],
        [
            pltpu.VMEM((N_WIDE, MROWS, 2 * HEAD), jnp.bfloat16),
            pltpu.VMEM(table, jnp.float32),
            pltpu.VMEM(table, jnp.bfloat16),
            pltpu.SemaphoreType.DMA((PACK_STEPS + 1,)),
        ],
        out=HBM,
    )
    slots = jnp.concatenate([owners, passage_counts])
    outgoing, slots = lax.optimization_barrier((outgoing, slots))
    arrived = lax.all_to_all(outgoing, WIDE, 0, 0, tiled=True)
    query_gradient, self_keyval_grads, memory_grads = attend(
        slots, arrived, query_states, output_grads, self_keyvals
    )
    returned = lax.all_to_all(memory_grads, WIDE, 0, 0, tiled=True)
    (passage_grads,) = kernel_call(
        collect_kernel,
        (wanted,),
        (returned, keyvals),
        [((P_DEV * MROWS + 16, 2 * HEAD), jnp.bfloat16)],
        [pltpu.VMEM((P_DEV + 1, MROWS, 2 * HEAD), jnp.float32)],
        limit=FEW,
    )
    all_heads = spread(passage_grads, "mp")
    last = (all_heads, weight, other_weight, passage_states, inverse)
    features = passage_states.shape[1]
    (gain_part,) = kernel_call(
        gain_kernel,
        (place,),
        last,
        [((1, features), jnp.float32)],
        flops=1 << 30,
        moved=6 << 20,
        limit=FEW,
    )
    gain_part = lax.psum(gain_part.reshape(-1, HEAD), "c").astype(jnp.bfloat16)
    gain_grads = jnp.sum(spread(gain_part, ("z", "y")).astype(jnp.float32), 0).reshape(-1)
    (state_grads,) = kernel_call(
        state_kernel,
        (place,),
        last + (norm_gain[None, :],),
        [(passage_states.shape, jnp.bfloat16)],
        flops=1 << 30,
        moved=7 << 20,
        limit=FEW,
    )
    return (state_grads, gain_grads, query_gradient, self_keyval_grads)


def solution(mesh):
    grid = Mesh(mesh.devices.reshape(8, 8, 2, 4), WIDE + ("mp",))
    in_specs = (
        P(WIDE, "mp"),
        P("mp"),
        P("mp", WIDE),
        P(WIDE, "mp"),
        P(WIDE, "mp"),
        P(WIDE, "mp"),
        P(WIDE, None),
        P(WIDE),
    )
    out_specs = (P(WIDE, "mp"), P("mp"), P(WIDE, "mp"), P(WIDE, "mp"))
    return jax.shard_map(
        on_device, mesh=grid, in_specs=in_specs, out_specs=out_specs, check_vma=False
    )
```

```python
import math

import jax
import jax.numpy as jnp
from jax import lax
from jax.experimental import pallas as pl
from jax.experimental.pallas import tpu as pltpu
from jax.sharding import Mesh
from jax.sharding import PartitionSpec as P

D = 8192
MROWS = 16
HEAD = 128
GROUP = 8
QLEN = 128
CAP = 32
MEM = CAP * MROWS
KEYS = MEM + QLEN
N_WIDE = 128
P_DEV = 16
EPSILON = 1e-05
SCALE = 1.0 / math.sqrt(HEAD)
LOG2E = math.log2(math.e)
FEW, MANY = 32 * 1024 * 1024, 60 * 1024 * 1024

NT = (((1,), (1,)), ((), ()))
TN = (((0,), (0,)), ((), ()))
SWAP = ((0, 1), (1, 0))
VMEM = pl.BlockSpec(memory_space=pltpu.VMEM)
SMEM = pl.BlockSpec(memory_space=pltpu.SMEM)
HBM = pl.BlockSpec(memory_space=pltpu.HBM)


def dot(a, b, dims=(((1,), (0,)), ((), ()))):
    return lax.dot_general(a, b, dims, preferred_element_type=jnp.float32)


def kernel_call(
    body, scalars, arrays, out_shapes, scratch=(), flops=1 << 20, moved=2 << 20, given=VMEM, out=VMEM, limit=MANY
):
    return pl.pallas_call(
        body,
        in_specs=[SMEM] * len(scalars) + [given] * len(arrays),
        out_specs=[out] * len(out_shapes),
        out_shape=[jax.ShapeDtypeStruct(*one) for one in out_shapes],
        scratch_shapes=list(scratch),
        compiler_params=pltpu.CompilerParams(vmem_limit_bytes=limit),
        cost_estimate=pl.CostEstimate(flops=flops, bytes_accessed=moved, transcendentals=0),
    )(*scalars, *arrays)


def wide_as(columns, width):
    return jnp.concatenate([columns] * (width // columns.shape[1]), axis=1)


def project_kernel(place_ref, rows_ref, weight_ref, *refs):
    *others, out_ref = refs
    half = rows_ref.shape[1] // 2
    rows = rows_ref[:, pl.ds(pl.multiple_of(place_ref[0] * half, half), half)]
    for h in range(out_ref.shape[0]):
        total = dot(rows, weight_ref[h * 2 * HEAD : (h + 1) * 2 * HEAD, :half], NT)
        for other in others:
            total = total + other[h]
        out_ref[h] = total.astype(out_ref.dtype)


def project(place, rows, weight, dtype, *others):
    shape = (weight.shape[0] // (2 * HEAD), rows.shape[0], 2 * HEAD)
    (sums,) = kernel_call(
        project_kernel,
        (place,),
        (rows, weight) + others,
        [(shape, dtype)],
        flops=1 << 29,
        moved=4 << 20,
        limit=FEW,
    )
    return sums


PACK_STEPS = 4


def pack_kernel(
    wanted_ref,
    parts_ref,
    out_hbm,
    keyvals_hbm,
    out_ref,
    keyvals_ref,
    table_ref,
    sems,
):
    total = parts_ref[0].astype(jnp.float32)
    for part in range(1, parts_ref.shape[0]):
        total = total + parts_ref[part].astype(jnp.float32)
    total = total.reshape(P_DEV, MROWS, 2 * HEAD)
    keyvals_ref[...] = total
    copies = [pltpu.make_async_copy(keyvals_ref, keyvals_hbm, sems.at[PACK_STEPS])]
    copies[0].start()
    table_ref[...] = total.astype(jnp.bfloat16)
    slots = N_WIDE // PACK_STEPS
    for step in range(PACK_STEPS):
        for slot in range(step * slots, (step + 1) * slots):
            out_ref[slot] = table_ref[jnp.maximum(wanted_ref[slot], 0)]
        done = pl.ds(step * slots, slots)
        copies.append(pltpu.make_async_copy(out_ref.at[done], out_hbm.at[done], sems.at[step]))
        copies[-1].start()
    for copy in copies:
        copy.wait()


def attend_kernel(
    slots_ref,
    arrived_hbm,
    query_hbm,
    grad_hbm,
    self_hbm,
    query_out_hbm,
    self_out_hbm,
    outgoing_hbm,
    arrived_ref,
    query_ref,
    grad_ref,
    self_ref,
    query_out,
    self_out,
    outgoing_ref,
    key_rows,
    value_rows,
    key_grads,
    value_grads,
    in_sems,
    out_sems,
    question_sems,
):
    loads = [
        pltpu.make_async_copy(source, target, in_sems.at[index])
        for index, (source, target) in enumerate(
            [
                (arrived_hbm, arrived_ref),
                (query_hbm, query_ref),
                (grad_hbm, grad_ref),
                (self_hbm, self_ref),
            ]
        )
    ]
    for load in loads:
        load.start()
    outgoing_ref[...] = jnp.zeros_like(outgoing_ref)
    for load in loads:
        load.wait()
    pair = 2 * QLEN
    key_index = lax.broadcasted_iota(jnp.int32, (MEM, pair), 0)
    self_index = lax.broadcasted_iota(jnp.int32, (QLEN, pair), 0)
    token = lax.broadcasted_iota(jnp.int32, (QLEN, pair), 1) % QLEN

    @pl.loop(0, query_ref.shape[0] // QLEN)
    def _(question):
        live = slots_ref[SLOTS + question]
        tokens = pl.ds(pl.multiple_of(question * QLEN, QLEN), QLEN)
        for k in range(CAP):
            slot = slots_ref[question * CAP + k]
            key_rows[k * MROWS : (k + 1) * MROWS, :] = arrived_ref[slot, :, :HEAD]
            value_rows[k * MROWS : (k + 1) * MROWS, :] = arrived_ref[slot, :, HEAD:]
        key_rows[MEM:, :] = self_ref[tokens, :HEAD]
        value_rows[MEM:, :] = self_ref[tokens, HEAD:]
        key_block = key_rows[...]
        value_block = value_rows[...]
        key_turned = key_block.T
        allowed = jnp.concatenate([key_index < live * MROWS, self_index <= token], axis=0)
        for g in range(0, GROUP, 2):
            first = slice(g * HEAD, (g + 1) * HEAD)
            second = slice((g + 1) * HEAD, (g + 2) * HEAD)
            queries = jnp.concatenate([query_ref[tokens, first], query_ref[tokens, second]], axis=0)
            grads = jnp.concatenate([grad_ref[tokens, first], grad_ref[tokens, second]], axis=0)
            scores = jnp.where(allowed, dot(key_block, queries, NT), -1e30)
            top = jnp.max(scores, axis=0, keepdims=True)
            exponent = jnp.exp2((scores - top) * (SCALE * LOG2E))
            probs = exponent * (1.0 / jnp.sum(exponent, axis=0, keepdims=True))
            rounded = probs.astype(jnp.bfloat16)
            prob_grads = dot(value_block, grads, NT)
            delta = jnp.sum(rounded.astype(jnp.float32) * prob_grads, axis=0, keepdims=True)
            score_grads = (probs * (prob_grads - delta) * SCALE).astype(jnp.bfloat16)
            value_part = dot(rounded, grads)
            key_part = dot(score_grads, queries)
            if g == 0:
                value_grads[...] = value_part
                key_grads[...] = key_part
            else:
                value_grads[...] += value_part
                key_grads[...] += key_part
            query_part = dot(key_turned, score_grads)
            query_out[tokens, first] = query_part[:, :QLEN].T
            query_out[tokens, second] = query_part[:, QLEN:].T
        pltpu.make_async_copy(
            query_out.at[tokens], query_out_hbm.at[tokens], question_sems.at[question]
        ).start()
        self_out[tokens, :HEAD] = key_grads[MEM:, :]
        self_out[tokens, HEAD:] = value_grads[MEM:, :]
        for k in range(CAP):
            slot = slots_ref[question * CAP + k]
            rows = slice(k * MROWS, (k + 1) * MROWS)

            @pl.when(k < live)
            def _():
                outgoing_ref[slot, :, :HEAD] = key_grads[rows, :].astype(jnp.bfloat16)
                outgoing_ref[slot, :, HEAD:] = value_grads[rows, :].astype(jnp.bfloat16)

    stores = [
        pltpu.make_async_copy(outgoing_ref, outgoing_hbm, out_sems.at[0]),
        pltpu.make_async_copy(self_out, self_out_hbm, out_sems.at[1]),
    ]
    for store in stores:
        store.start()
    for question in range(query_ref.shape[0] // QLEN):
        tokens = pl.ds(question * QLEN, QLEN)
        stores.append(
            pltpu.make_async_copy(
                query_out.at[tokens], query_out_hbm.at[tokens], question_sems.at[question]
            )
        )
    for store in stores:
        store.wait()


def attend(slots, arrived, queries, grads, self_rows):
    return kernel_call(
        attend_kernel,
        (slots,),
        (arrived, queries, grads, self_rows),
        [
            (queries.shape, jnp.float32),
            (self_rows.shape, jnp.float32),
            (arrived.shape, jnp.bfloat16),
        ],
        [
            pltpu.VMEM(arrived.shape, jnp.bfloat16),
            pltpu.VMEM(queries.shape, jnp.bfloat16),
            pltpu.VMEM(grads.shape, jnp.bfloat16),
            pltpu.VMEM(self_rows.shape, jnp.bfloat16),
            pltpu.VMEM(queries.shape, jnp.float32),
            pltpu.VMEM(self_rows.shape, jnp.float32),
            pltpu.VMEM(arrived.shape, jnp.bfloat16),
        ]
        + [pltpu.VMEM((KEYS, HEAD), jnp.bfloat16)] * 2
        + [pltpu.VMEM((KEYS, HEAD), jnp.float32)] * 2
        + [pltpu.SemaphoreType.DMA((4,)), pltpu.SemaphoreType.DMA((2,)), pltpu.SemaphoreType.DMA((2,))],
        flops=2 << 30,
        moved=5 << 20,
        given=HBM,
        out=HBM,
    )


def collect_kernel(wanted_ref, returned_ref, keyvals_ref, out_ref, sums):
    sums[...] = jnp.zeros_like(sums)
    for slot in range(N_WIDE):
        row = wanted_ref[slot]
        sums[jnp.where(row < 0, P_DEV, row)] += returned_ref[slot].astype(jnp.float32)
    total = P_DEV * MROWS
    rounded = sums[:P_DEV].reshape(total, 2 * HEAD).astype(jnp.bfloat16)
    products = rounded.astype(jnp.float32) * keyvals_ref[...].reshape(total, 2 * HEAD)
    inner = lax.dot_general(
        jnp.ones((8, 2 * HEAD), jnp.float32),
        products,
        NT,
        precision=lax.Precision.HIGHEST,
        preferred_element_type=jnp.float32,
    )
    high = inner.astype(jnp.bfloat16)
    low = (inner - high.astype(jnp.float32)).astype(jnp.bfloat16)
    out_ref[:total, :] = rounded
    out_ref[total:, :] = jnp.concatenate([high, low], axis=0)


BLOCK = 256


def row_blocks(place_ref, all_heads_ref, weight_refs, states_ref, inverse_ref, finish):
    core = place_ref[0]
    total, features = states_ref.shape
    half = features // 2
    inverse = wide_as(inverse_ref[...], BLOCK)
    for place in range(2):
        start = (core if place == 0 else 1 - core) * half
        for block in range(half // BLOCK):
            span = slice(block * BLOCK, (block + 1) * BLOCK)
            row_grads = None
            for h in range(all_heads_ref.shape[0]):
                weight = weight_refs[place][h * 2 * HEAD : (h + 1) * 2 * HEAD, span]
                part = dot(all_heads_ref[h, :total, :], weight)
                row_grads = part if row_grads is None else row_grads + part
            lanes = pl.ds(pl.multiple_of(start + block * BLOCK, BLOCK), BLOCK)
            normed = states_ref[:, lanes].astype(jnp.float32) * inverse
            finish(lanes, row_grads, normed, inverse)


def gain_kernel(place_ref, all_heads_ref, w0, w1, states_ref, inverse_ref, out_ref):
    def finish(lanes, row_grads, normed, inverse):
        out_ref[:, lanes] = jnp.sum(row_grads * normed, axis=0, keepdims=True)

    row_blocks(place_ref, all_heads_ref, (w0, w1), states_ref, inverse_ref, finish)


def state_kernel(place_ref, all_heads_ref, w0, w1, states_ref, inverse_ref, gain_ref, out_ref):
    total = states_ref.shape[0]
    heads = all_heads_ref.shape[0]
    extra = jnp.concatenate([all_heads_ref[h, total:, :] for h in range(heads)], axis=0)
    share = jnp.full((extra.shape[0], HEAD), 1.0 / (8 * D), jnp.bfloat16)
    mean = wide_as(dot(extra, share, TN), BLOCK)

    def finish(lanes, row_grads, normed, inverse):
        scaled = row_grads * gain_ref[:, lanes]
        out_ref[:, lanes] = (inverse * (scaled - normed * mean)).astype(jnp.bfloat16)

    row_blocks(place_ref, all_heads_ref, (w0, w1), states_ref, inverse_ref, finish)


def spread(array, axis):
    count = lax.axis_size(axis)
    copies = jnp.broadcast_to(array[None], (count,) + array.shape)
    return lax.all_to_all(copies, axis, 0, 0, tiled=True)


WIDE = ("z", "y", "c")
SLOTS = 2 * CAP


def on_device(
    passage_states,
    norm_gain,
    proj_weight,
    query_states,
    self_keyvals,
    output_grads,
    passage_ids,
    passage_counts,
):
    core = lax.axis_index("c")
    place = jnp.stack([core, 1 - core]).astype(jnp.int32)
    me = lax.axis_index(WIDE)
    half = passage_states.shape[1] // 2

    live = jnp.arange(CAP, dtype=jnp.int32)[None, :] < passage_counts[:, None]
    owners = jnp.where(live, passage_ids // P_DEV, 0).reshape(-1)
    places = jnp.where(live, passage_ids % P_DEV + 1, 0).reshape(-1)
    hits = owners[:, None] == jnp.arange(N_WIDE)[None, :]
    requests = jnp.sum(jnp.where(hits, places[:, None], 0), 0).astype(jnp.bfloat16)

    turned = proj_weight.T
    columns = turned.shape[0]
    halves = jnp.transpose(turned.reshape(columns, 2, half), (1, 0, 2))
    block = lax.all_to_all(halves, "c", 0, 0, tiled=True).reshape(2 * columns, half)
    ridden = jnp.broadcast_to(requests[None], (2 * columns, N_WIDE))
    blob = jnp.concatenate([block, ridden], axis=1)
    blob = spread(blob, ("z", "y")).reshape(-1, half + N_WIDE)

    states = passage_states.astype(jnp.float32)
    squares = lax.psum(jnp.sum(states * states, 1), "mp")
    inverse_rms = lax.rsqrt(squares / D + EPSILON)[:, None]
    memory_rows = (states * inverse_rms * norm_gain).astype(jnp.bfloat16)
    inverse = jnp.broadcast_to(inverse_rms, (inverse_rms.shape[0], HEAD))
    weight, memory_rows, inverse = lax.optimization_barrier((blob, memory_rows, inverse))

    other_weight = lax.ppermute(weight, "c", SWAP)
    own_sums = project(place, memory_rows, weight, jnp.float32)
    partial_sums = project(place[::-1], memory_rows, other_weight, jnp.bfloat16, own_sums)
    wanted = []
    for tables in (weight, other_weight):
        tables = tables.reshape(-1, 2 * columns, half + N_WIDE)[:, 0, half:].astype(jnp.int32)
        wanted.append(jnp.sum(jnp.where(jnp.arange(N_WIDE)[None, :] == me, tables, 0), 1) - 1)
    ours, theirs = wanted
    wanted = jnp.where(core == 0, jnp.stack([ours, theirs], 1), jnp.stack([theirs, ours], 1))
    wanted = wanted.reshape(-1)
    parts = lax.all_to_all(partial_sums, "mp", 0, 0, tiled=True)
    parts, wanted = lax.optimization_barrier((parts, wanted))
    table = (P_DEV, MROWS, 2 * HEAD)
    outgoing, keyvals = kernel_call(
        pack_kernel,
        (wanted,),
        (parts,),
        [((N_WIDE, MROWS, 2 * HEAD), jnp.bfloat16), (table, jnp.float32)],
        [
            pltpu.VMEM((N_WIDE, MROWS, 2 * HEAD), jnp.bfloat16),
            pltpu.VMEM(table, jnp.float32),
            pltpu.VMEM(table, jnp.bfloat16),
            pltpu.SemaphoreType.DMA((PACK_STEPS + 1,)),
        ],
        out=HBM,
    )
    slots = jnp.concatenate([owners, passage_counts])
    outgoing, slots = lax.optimization_barrier((outgoing, slots))
    arrived = lax.all_to_all(outgoing, WIDE, 0, 0, tiled=True)
    query_gradient, self_keyval_grads, memory_grads = attend(
        slots, arrived, query_states, output_grads, self_keyvals
    )
    returned = lax.all_to_all(memory_grads, WIDE, 0, 0, tiled=True)
    (passage_grads,) = kernel_call(
        collect_kernel,
        (wanted,),
        (returned, keyvals),
        [((P_DEV * MROWS + 16, 2 * HEAD), jnp.bfloat16)],
        [pltpu.VMEM((P_DEV + 1, MROWS, 2 * HEAD), jnp.float32)],
        limit=FEW,
    )
    all_heads = spread(passage_grads, "mp")
    last = (all_heads, weight, other_weight, passage_states, inverse)
    features = passage_states.shape[1]
    (gain_part,) = kernel_call(
        gain_kernel,
        (place,),
        last,
        [((1, features), jnp.float32)],
        flops=1 << 30,
        moved=6 << 20,
        limit=FEW,
    )
    gain_part = lax.psum(gain_part.reshape(-1, HEAD), "c").astype(jnp.bfloat16)
    gain_grads = jnp.sum(spread(gain_part, ("z", "y")).astype(jnp.float32), 0).reshape(-1)
    (state_grads,) = kernel_call(
        state_kernel,
        (place,),
        last + (norm_gain[None, :],),
        [(passage_states.shape, jnp.bfloat16)],
        flops=1 << 30,
        moved=7 << 20,
        limit=FEW,
    )
    return (state_grads, gain_grads, query_gradient, self_keyval_grads)


def solution(mesh):
    grid = Mesh(mesh.devices.reshape(8, 8, 2, 4), WIDE + ("mp",))
    in_specs = (
        P(WIDE, "mp"),
        P("mp"),
        P("mp", WIDE),
        P(WIDE, "mp"),
        P(WIDE, "mp"),
        P(WIDE, "mp"),
        P(WIDE, None),
        P(WIDE),
    )
    out_specs = (P(WIDE, "mp"), P("mp"), P(WIDE, "mp"), P(WIDE, "mp"))
    return jax.shard_map(
        on_device, mesh=grid, in_specs=in_specs, out_specs=out_specs, check_vma=False
    )
```
